32 devices in a mesh: groups: 2 (over y), gx: 8 (over z, x), gy: 2 (over core).
Axes of the slice: x: 2, y: 2, z: 4, core: 2. Of those that a mesh axis runs over, the one named last changes fastest.
Arguments:
- x_in: bfloat16 [256, 4672], P(('groups', 'gx'), 'gy'), parts along dimension 0, may hold values from -6 to 6
- lengths: int32 [256], P(('groups', 'gy')), parts along dimension 0, may hold values from 32 to 128, as said below
- self_gain: float32 [4672], P('gy'), may hold values from 0.1 to 1.9
- cross_gain: float32 [4672], P('gy'), may hold values from 0.1 to 1.9
- ffn_gain: float32 [4672], P('gy'), may hold values from 0.1 to 1.9
- final_gain: float32 [4672], P('gy'), may hold values from 0.1 to 1.9
- self_query: bfloat16 [4672, 4096], P('gy', 'gx'), may hold values from -0.01171875 to 0.01171875
- self_kv: bfloat16 [4672, 64, 128], P('gy', 'gx'), may hold values from -0.09375 to 0.09375
- self_out: bfloat16 [4096, 4672], P('gx', 'gy'), may hold values from -0.09375 to 0.09375
- cross_query: bfloat16 [4672, 4096], P('gy', 'gx'), may hold values from -0.01171875 to 0.01171875
- cross_out: bfloat16 [4096, 4672], P('gx', 'gy'), may hold values from -0.09375 to 0.09375
- ffn_gate: bfloat16 [4672, 12352], P('gy', 'gx'), may hold values from -0.09375 to 0.09375
- ffn_up: bfloat16 [4672, 12352], P('gy', 'gx'), may hold values from -0.09375 to 0.09375
- ffn_down: bfloat16 [12352, 4672], P('gx', 'gy'), may hold values from -0.0546875 to 0.0546875
- self_keys: bfloat16 [64, 256, 64, 128], P('gx', ('groups', 'gy')), parts along dimension 1, may hold values from -1500 to 1500
- self_values: bfloat16 [64, 256, 64, 128], P('gx', ('groups', 'gy')), parts along dimension 1, may hold values from -6 to 6
- cross_keys: bfloat16 [64, 256, 64, 128], P('gx', ('groups', 'gy')), parts along dimension 1, may hold values from -1500 to 1500
- cross_values: bfloat16 [64, 256, 64, 128], P('gx', ('groups', 'gy')), parts along dimension 1, may hold values from -6 to 6
Outputs:
- decoded: bfloat16 [256, 4672], P(('groups', 'gx'), 'gy'), parts along dimension 0
The draws below stay inside these ranges and needn't reach their ends.
There are 2 independent parts, one for each index of `groups`. The reference program is written for one: setup_inputs(seed, part) draws one part's arguments, and reference() takes and returns one part's arrays. A program takes and returns all parts, laid end to end along the dimension named above; an argument that names none is the same for every part. Nothing has to cross between parts.
Inputs may be any that keep to these rules, and one draw needn't show every extreme that they name: lengths[b] counts the filled slots of row b's self-attention cache, slots 0 to lengths[b] - 1; in every draw some row fills all 128 slots.
All inputs are finite; a program needn't handle non-finite values.
Results may differ from the reference program's by a relative error of at most 0.02.
The reference program's roundings to bfloat16 on the way count: a program that leaves them out, or rounds other values in their place, can miss the bound.
Values may be sent and summed in bfloat16 or wider, within the bound.
No kernel may reach another device: no remote copies, remote signals or barrier semaphores. Data moves between devices by JAX's collectives and lax.ppermute only.
A program may use at most 192 MiB of HBM per device.

```python
import math
from functools import partial
import jax
import jax.numpy as jnp
from jax import lax

D = 4672
NH = 64
DK = 64
FF = 12352
ROWS = 128
SELF = 128
MEM = 128


def slot_scales(key, length):
    return jnp.exp(jax.random.uniform(key, (1, 1, 1, length), jnp.float32, math.log(0.3), math.log(3.0)))


def draw_lengths(key, part):
    key = jax.random.fold_in(key, 7)
    key_fill, key_row = jax.random.split(key)
    filled = jax.random.randint(key_fill, (ROWS,), SELF // 4, SELF + 1)
    full_row = jax.random.randint(key_row, (), 0, ROWS)
    positions = lax.broadcasted_iota(jnp.int32, (ROWS,), 0)
    return jnp.where(positions == full_row, SELF, filled).astype(jnp.int32)


def draw_self_keys(key, part):
    key = jax.random.fold_in(key, 11)
    key_law, key_scale = jax.random.split(key, 2)
    raw = jax.random.normal(key_law, (NH, ROWS, DK, SELF), jnp.float32) * slot_scales(key_scale, SELF)
    return raw.astype(jnp.bfloat16)


def draw_cross_keys(key, part):
    key = jax.random.fold_in(key, 23)
    key_law, key_scale = jax.random.split(key, 2)
    raw = jax.random.normal(key_law, (NH, ROWS, DK, MEM), jnp.float32) * slot_scales(key_scale, MEM)
    return raw.astype(jnp.bfloat16)


def levels(stream_key, dims, shards, least, high):
    def one(dim, parts):
        heights = jax.random.uniform(jax.random.fold_in(jax.random.fold_in(stream_key, 6), dim), (parts,), jnp.float32, least / len(shards), high / len(shards))
        return jnp.repeat(jnp.exp(heights), dims[dim] // parts).reshape((-1,) + (1,) * (len(dims) - dim - 1))

    loudness = one(*shards[0])
    for cut in shards[1:]:
        loudness = loudness * one(*cut)
    return loudness


def normal_values(own_key, dims, scale, most, cuts=(), dtype=jnp.bfloat16):
    level = levels(own_key, dims, cuts, -0.22, 0.18) if cuts else 1.0
    values = jax.random.normal(own_key, dims, jnp.float32) * scale * level
    return jnp.minimum(jnp.maximum(values, -most), most).astype(dtype)


def setup_inputs(seed: int = 0, part: int = 0) -> dict:
    key_list = jax.random.split(jax.random.key(seed), 19)
    part_keys = jax.random.split(jax.random.fold_in(key_list[18], part), 19)
    return {
        "x_in": normal_values(part_keys[0], (ROWS, D), 1.0, 6.0, ((0, 8), (1, 2))),
        "lengths": draw_lengths(jax.random.fold_in(jax.random.fold_in(key_list[18], part), 71), part),
        "self_gain": jnp.clip(1.0 + 0.18 * jax.random.normal(key_list[2], (D,), jnp.float32), 0.1, 1.9),
        "cross_gain": jnp.clip(1.0 + 0.18 * jax.random.normal(key_list[3], (D,), jnp.float32), 0.1, 1.9),
        "ffn_gain": jnp.clip(1.0 + 0.18 * jax.random.normal(key_list[4], (D,), jnp.float32), 0.1, 1.9),
        "final_gain": jnp.clip(1.0 + 0.18 * jax.random.normal(key_list[5], (D,), jnp.float32), 0.1, 1.9),
        "self_query": normal_values(key_list[6], (D, NH * DK), (D * DK) ** -0.5, 0.01171875, ((0, 2), (1, 8))),
        "self_kv": normal_values(key_list[7], (D, NH, 2 * DK), D ** -0.5, 0.09375, ((0, 2), (1, 8))),
        "self_out": normal_values(key_list[8], (NH * DK, D), (NH * DK) ** -0.5, 0.09375, ((0, 8), (1, 2))),
        "cross_query": normal_values(key_list[9], (D, NH * DK), (D * DK) ** -0.5, 0.01171875, ((0, 2), (1, 8))),
        "cross_out": normal_values(key_list[10], (NH * DK, D), (NH * DK) ** -0.5, 0.09375, ((0, 8), (1, 2))),
        "ffn_gate": normal_values(key_list[11], (D, FF), D ** -0.5, 0.09375, ((0, 2), (1, 8))),
        "ffn_up": normal_values(key_list[12], (D, FF), D ** -0.5, 0.09375, ((0, 2), (1, 8))),
        "ffn_down": normal_values(key_list[13], (FF, D), FF ** -0.5, 0.0546875, ((0, 8), (1, 2))),
        "self_keys": draw_self_keys(jax.random.fold_in(jax.random.fold_in(key_list[18], part), 71), part),
        "self_values": normal_values(part_keys[15], (NH, ROWS, DK, SELF), 1.0, 6.0, ((0, 8), (1, 2))),
        "cross_keys": draw_cross_keys(jax.random.fold_in(jax.random.fold_in(key_list[18], part), 71), part),
        "cross_values": normal_values(part_keys[17], (NH, ROWS, DK, MEM), 1.0, 6.0, ((0, 8), (1, 2))),
    }


def rms_norm(stream, gain):
    stream_f = stream.astype(jnp.float32)
    inverse = lax.rsqrt(lax.optimization_barrier(jnp.sum(stream_f * stream_f, axis=1)) / D + 1e-06)
    return (stream_f * inverse[:, None] * gain.astype(jnp.float32)[None, :]).astype(jnp.bfloat16)

def self_head(lengths, operands):
    query, new_key, new_value, cache_keys, cache_values = operands
    query_f = query.astype(jnp.float32)
    scores = jnp.einsum('bd,bds->bs', query_f, cache_keys.astype(jnp.float32))
    own_score = lax.optimization_barrier(jnp.sum(query_f * new_key.astype(jnp.float32), axis=1))
    slots = lax.broadcasted_iota(jnp.int32, scores.shape, 1)
    valid_slots = slots < lengths[:, None]
    scores = jnp.where(valid_slots, scores, -1e+30)
    top_score = jnp.maximum(lax.optimization_barrier(jnp.max(scores, axis=1)), own_score)
    expo = jnp.where(valid_slots, jnp.exp(scores - top_score[:, None]), 0.0)
    own_expo = jnp.exp(own_score - top_score)
    totals = lax.optimization_barrier(jnp.sum(expo, axis=1)) + own_expo
    attn_probs = (expo / totals[:, None]).astype(jnp.bfloat16)
    own_prob = (own_expo / totals).astype(jnp.bfloat16)
    mixed = jnp.einsum('bs,bds->bd', attn_probs.astype(jnp.float32), cache_values.astype(jnp.float32))
    mixed = mixed + own_prob.astype(jnp.float32)[:, None] * new_value.astype(jnp.float32)
    return mixed.astype(jnp.bfloat16)

def cross_head(operands):
    query, cache_keys, cache_values = operands
    scores = jnp.einsum('bd,bds->bs', query.astype(jnp.float32), cache_keys.astype(jnp.float32))
    top_score = lax.optimization_barrier(jnp.max(scores, axis=1))
    expo = jnp.exp(scores - top_score[:, None])
    totals = lax.optimization_barrier(jnp.sum(expo, axis=1))
    attn_probs = (expo / totals[:, None]).astype(jnp.bfloat16)
    mixed = jnp.einsum('bs,bds->bd', attn_probs.astype(jnp.float32), cache_values.astype(jnp.float32))
    return mixed.astype(jnp.bfloat16)

def reference(x_in, lengths, self_gain, cross_gain, ffn_gain, final_gain, self_query, self_kv, self_out, cross_query, cross_out, ffn_gate, ffn_up, ffn_down, self_keys, self_values, cross_keys, cross_values):
    normed = rms_norm(x_in, self_gain)
    query = jnp.dot(normed, self_query, preferred_element_type=jnp.float32).astype(jnp.bfloat16)
    query = query.reshape(ROWS, NH, DK).transpose(1, 0, 2)
    new_kv = jnp.dot(normed, self_kv.reshape(D, NH * 2 * DK), preferred_element_type=jnp.float32).astype(jnp.bfloat16)
    new_kv = new_kv.reshape(ROWS, NH, 2 * DK).transpose(1, 0, 2)
    heads = lax.map(partial(self_head, lengths), (query, new_kv[:, :, :DK], new_kv[:, :, DK:], self_keys, self_values))
    heads = heads.transpose(1, 0, 2).reshape(ROWS, NH * DK)
    stream = (x_in.astype(jnp.float32) + jnp.dot(heads, self_out, preferred_element_type=jnp.float32)).astype(jnp.bfloat16)
    normed = rms_norm(stream, cross_gain)
    query = jnp.dot(normed, cross_query, preferred_element_type=jnp.float32).astype(jnp.bfloat16)
    query = query.reshape(ROWS, NH, DK).transpose(1, 0, 2)
    heads = lax.map(cross_head, (query, cross_keys, cross_values))
    heads = heads.transpose(1, 0, 2).reshape(ROWS, NH * DK)
    stream = (stream.astype(jnp.float32) + jnp.dot(heads, cross_out, preferred_element_type=jnp.float32)).astype(jnp.bfloat16)
    normed = rms_norm(stream, ffn_gain)
    gate_sum = jnp.dot(normed, ffn_gate, preferred_element_type=jnp.float32)
    up_sum = jnp.dot(normed, ffn_up, preferred_element_type=jnp.float32)
    hidden = (jax.nn.gelu(gate_sum, approximate=True) * up_sum).astype(jnp.bfloat16)
    stream = (stream.astype(jnp.float32) + jnp.dot(hidden, ffn_down, preferred_element_type=jnp.float32)).astype(jnp.bfloat16)
    return rms_norm(stream, final_gain)
```

```python
import jax
import jax.numpy as jnp
from jax import lax
from jax.sharding import PartitionSpec as P

D = 4672
DK = 64
F32 = jnp.float32
BF16 = jnp.bfloat16


def swap(value, axis, mask, size):
    return lax.ppermute(value, axis, [(i, i ^ mask) for i in range(size)])


class Line:
    def __init__(self, size):
        self.size = size
        self.direct = size == 8
        self.index = lax.axis_index("gx")

    def gather(self, block):
        if not self.direct:
            return lax.all_gather(block, "gx", axis=0, tiled=True)
        blocks = {0: block}
        for mask in (4, 6, 2):
            blocks[mask] = swap(block, "gx", mask, self.size)
        blocks[1] = swap(block, "gx", 1, self.size)
        for mask in (4, 2, 6):
            blocks[mask ^ 1] = swap(blocks[mask], "gx", 1, self.size)
        return jnp.concatenate([blocks[p] for p in range(self.size)], axis=0)

    def scatter_sum(self, partial):
        if not self.direct:
            return lax.psum_scatter(partial, "gx", scatter_dimension=0, tiled=True)
        rows = partial.shape[0] // self.size
        blocks = [partial[p * rows : (p + 1) * rows] for p in range(self.size)]
        pairs = {}
        for p in (6, 4, 2, 0):
            pairs[p] = blocks[p] + swap(blocks[p ^ 1].astype(BF16), "gx", 1, self.size).astype(F32)
        total = pairs[0]
        for mask in (6, 4, 2):
            total = total + swap(pairs[mask].astype(BF16), "gx", mask, self.size).astype(F32)
        return total

    def halves(self, value):
        gy = lax.axis_index("gy")
        half = value.shape[0] // 2
        first = gy ^ (self.index // 4) if self.direct else gy
        mine = jnp.where(first == 0, value[:half], value[half:])
        other = jnp.where(first == 0, value[half:], value[:half])
        return mine, other

    def join(self, mine, other):
        gy = lax.axis_index("gy")
        first = gy ^ (self.index // 4) if self.direct else gy
        low = jnp.where(first == 0, mine, other)
        high = jnp.where(first == 0, other, mine)
        return jnp.concatenate([low, high], axis=0)

    def reorder(self, half):
        if not self.direct:
            return half
        blocks = half.reshape(4, half.shape[0] // 4, half.shape[1])
        low = self.index & 3
        blocks = jnp.where(low & 1 == 0, blocks, blocks[jnp.array([1, 0, 3, 2])])
        blocks = jnp.where(low & 2 == 0, blocks, blocks[jnp.array([2, 3, 0, 1])])
        return blocks.reshape(half.shape)


def self_attend(query, new_key, new_value, cache_keys, cache_values, lengths):
    scores = jnp.einsum("bhd,hbds->hbs", query, cache_keys, preferred_element_type=jnp.float32)
    own_score = jnp.einsum("bhd,bhd->hb", query, new_key, preferred_element_type=jnp.float32)
    slots = lax.broadcasted_iota(jnp.int32, (1, scores.shape[1], scores.shape[2]), 2)
    valid_slots = slots < lengths[None, :, None]
    scores = jnp.where(valid_slots, scores, -1e30)
    top_score = jnp.maximum(jnp.max(scores, axis=2), own_score)
    expo = jnp.where(valid_slots, jnp.exp(scores - top_score[:, :, None]), 0.0)
    own_expo = jnp.exp(own_score - top_score)
    totals = jnp.sum(expo, axis=2) + own_expo
    attn_probs = (expo / totals[:, :, None]).astype(jnp.bfloat16)
    own_prob = (own_expo / totals).astype(jnp.bfloat16)
    mixed = jnp.einsum(
        "hbs,hbds->bhd", attn_probs, cache_values, preferred_element_type=jnp.float32
    )
    mixed = mixed + own_prob.T.astype(jnp.float32)[:, :, None] * new_value.astype(jnp.float32)
    return mixed.astype(jnp.bfloat16).reshape(query.shape[0], query.shape[1] * query.shape[2])


def cross_attend(query, cache_keys, cache_values):
    scores = jnp.einsum("bhd,hbds->hbs", query, cache_keys, preferred_element_type=jnp.float32)
    top_score = jnp.max(scores, axis=2)
    expo = jnp.exp(scores - top_score[:, :, None])
    totals = jnp.sum(expo, axis=2)
    attn_probs = (expo / totals[:, :, None]).astype(jnp.bfloat16)
    mixed = jnp.einsum(
        "hbs,hbds->bhd", attn_probs, cache_values, preferred_element_type=jnp.float32
    )
    return mixed.astype(jnp.bfloat16).reshape(query.shape[0], query.shape[1] * query.shape[2])


def normalize(stream, gain):
    stream_f = stream.astype(F32)
    squares = jnp.sum(stream_f * stream_f, axis=1, keepdims=True)
    squares = squares + swap(squares, "gy", 1, 2)
    inverse = lax.rsqrt(squares / D + 1e-06)
    return (stream_f * inverse * gain[None, :]).astype(BF16)


def dot(left, right):
    return jnp.dot(left, right, preferred_element_type=F32)


def per_device(
    size,
    x_in,
    lengths,
    self_gain,
    cross_gain,
    ffn_gain,
    final_gain,
    self_query,
    self_kv,
    self_out,
    cross_query,
    cross_out,
    ffn_gate,
    ffn_up,
    ffn_down,
    self_keys,
    self_values,
    cross_keys,
    cross_values,
):
    line = Line(size)
    width_local = x_in.shape[1]
    heads_here = self_query.shape[1] // DK
    rows_here = self_keys.shape[1]

    def half_sum(partial):
        mine, other = line.halves(partial)
        return mine + swap(other, "gy", 1, 2)

    def update(stream, partial):
        return (stream.astype(F32) + line.scatter_sum(partial)).astype(BF16)

    def project_heads(stream, heads, weight):
        heads = line.reorder(heads)
        return update(stream, dot(line.join(heads, swap(heads, "gy", 1, 2)), weight))

    stream = x_in
    normed = line.gather(normalize(stream, self_gain))
    query_part = dot(normed, self_query)
    pair_part = dot(normed, self_kv.reshape(width_local, heads_here * 2 * DK))
    query = line.reorder(half_sum(query_part)).astype(BF16).reshape(rows_here, heads_here, DK)
    new_pair = line.reorder(half_sum(pair_part)).astype(BF16).reshape(rows_here, heads_here, 2 * DK)
    heads = self_attend(
        query, new_pair[:, :, :DK], new_pair[:, :, DK:], self_keys, self_values, lengths
    )
    stream = project_heads(stream, heads, self_out)

    normed = line.gather(normalize(stream, cross_gain))
    query = line.reorder(half_sum(dot(normed, cross_query)))
    query = query.astype(BF16).reshape(rows_here, heads_here, DK)
    stream = project_heads(stream, cross_attend(query, cross_keys, cross_values), cross_out)

    normed = line.gather(normalize(stream, ffn_gain))
    gate = dot(normed, ffn_gate)
    gate = gate + swap(gate.astype(BF16), "gy", 1, 2).astype(F32)
    up = dot(normed, ffn_up)
    up = up + swap(up.astype(BF16), "gy", 1, 2).astype(F32)
    hidden = (jax.nn.gelu(gate, approximate=True) * up).astype(BF16)
    stream = update(stream, dot(hidden, ffn_down))
    return normalize(stream, final_gain)


def solution(mesh):
    size = mesh.shape["gx"]

    def device(*args):
        return per_device(size, *args)

    return jax.shard_map(
        device,
        mesh=mesh,
        in_specs=(
            P(("groups", "gx"), "gy"),
            P(("groups", "gy")),
            P("gy"),
            P("gy"),
            P("gy"),
            P("gy"),
            P("gy", "gx"),
            P("gy", "gx", None),
            P("gx", "gy"),
            P("gy", "gx"),
            P("gx", "gy"),
            P("gy", "gx"),
            P("gy", "gx"),
            P("gx", "gy"),
            P("gx", ("groups", "gy"), None, None),
            P("gx", ("groups", "gy"), None, None),
            P("gx", ("groups", "gy"), None, None),
            P("gx", ("groups", "gy"), None, None),
        ),
        out_specs=P(("groups", "gx"), "gy"),
        check_vma=False,
    )
```

```python
import jax
import jax.numpy as jnp
from jax import lax
from jax.experimental import pallas as pl
from jax.experimental.pallas import tpu as pltpu
from jax.sharding import PartitionSpec as P

D = 4672
DK = 64
F32 = jnp.float32
BF16 = jnp.bfloat16
VMEM = pl.BlockSpec(memory_space=pltpu.VMEM)
SMEM = pl.BlockSpec(memory_space=pltpu.SMEM)
ANY = pl.BlockSpec(memory_space=pl.ANY)
NT = (((1,), (1,)), ((), ()))


def swap(value, axis, mask, size):
    return lax.ppermute(value, axis, [(i, i ^ mask) for i in range(size)])


def dot(left, right):
    return jnp.dot(left, right, preferred_element_type=F32)


def pieces(total, step):
    starts = list(range(0, total, step))
    if total - starts[-1] < step // 8 and len(starts) > 1:
        starts.pop()
    return [(s, e - s) for s, e in zip(starts, starts[1:] + [total])]


def normalize(stream, gain):
    stream_f = stream.astype(F32)
    squares = jnp.sum(stream_f * stream_f, axis=1, keepdims=True)
    squares = squares + swap(squares, "gy", 1, 2)
    inverse = lax.rsqrt(squares / D + 1e-06)
    return (stream_f * inverse * gain[None, :]).astype(BF16)


def gather_blocks(block):
    blocks = {0: block}
    for mask in (4, 6, 2):
        blocks[mask] = swap(block, "gx", mask, 8)
    blocks[1] = swap(block, "gx", 1, 8)
    for mask in (4, 2, 6):
        blocks[mask ^ 1] = swap(blocks[mask], "gx", 1, 8)
    return [blocks[p] for p in range(8)]


def scatter_sum(kept, sent):
    pairs = {}
    for k in (3, 2, 1, 0):
        pairs[k] = kept[k] + swap(sent[k], "gx", 1, 8).astype(F32)
    total = pairs[0]
    for k in (3, 2, 1):
        total = total + swap(pairs[k].astype(BF16), "gx", 2 * k, 8).astype(F32)
    return total


def store_blocks(result, kept, sent, start, length):
    rows = kept[0].shape[0]
    for k in range(4):
        low = 2 * k * rows
        kept[k][:, start : start + length] = result[low : low + rows]
        sent[k][:, start : start + length] = result[low + rows : low + 2 * rows].astype(BF16)


def block_shapes(rows, width):
    return [jax.ShapeDtypeStruct((rows, width), F32)] * 4 + [
        jax.ShapeDtypeStruct((rows, width), BF16)
    ] * 4


def heads_out_kernel(cuts, first, mine, other, weight, *rest):
    kept, sent, (held, sems) = rest[:4], rest[4:8], rest[8:]
    copies = [
        pltpu.make_async_copy(weight.at[pl.ds(s, n)], held.at[pl.ds(s, n)], sems.at[i])
        for i, (s, n) in enumerate(cuts)
    ]
    for copy in copies:
        copy.start()
    swapped = first[0] == 1
    a, b = mine[...], other[...]
    left = jnp.concatenate([jnp.where(swapped, b, a), jnp.where(swapped, a, b)], axis=0)
    for copy, (s, n) in zip(copies, cuts):
        copy.wait()
        result = lax.dot_general(left, held[pl.ds(s, n), :], NT, preferred_element_type=F32)
        store_blocks(result, kept, sent, s, n)


def heads_out(first, mine, other, weight_t):
    width, depth = weight_t.shape
    cuts = pieces(width, 512)
    outs = pl.pallas_call(
        lambda *refs: heads_out_kernel(cuts, *refs),
        out_shape=block_shapes(mine.shape[0] // 4, width),
        in_specs=[SMEM, VMEM, VMEM, ANY],
        out_specs=[VMEM] * 8,
        scratch_shapes=[
            pltpu.VMEM((width, depth), BF16),
            pltpu.SemaphoreType.DMA((len(cuts),)),
        ],
        compiler_params=pltpu.CompilerParams(vmem_limit_bytes=16 << 20),
        name="heads_out",
    )(first, mine, other, weight_t)
    return outs[:4], outs[4:]


def arranged(first, blocks):
    swapped = first[0] == 1
    low = jnp.concatenate([b[...] for b in blocks[:4]], axis=0)
    high = jnp.concatenate([b[...] for b in blocks[4:]], axis=0)
    return jnp.concatenate([jnp.where(swapped, high, low), jnp.where(swapped, low, high)], axis=0)


def query_kernel(cuts, first, *rest):
    blocks, (weight, mine, other, left, held, sems) = rest[:8], rest[8:]
    copies = [
        pltpu.make_async_copy(weight.at[pl.ds(s, n)], held.at[pl.ds(s, n)], sems.at[i])
        for i, (s, n) in enumerate(cuts)
    ]
    for copy in copies:
        copy.start()
    left[...] = arranged(first, blocks)
    total = None
    for copy, (s, n) in zip(copies, cuts):
        copy.wait()
        part = dot(left[:, s : s + n], held[pl.ds(s, n), :])
        total = part if total is None else total + part
    half = mine.shape[0]
    mine[...] = total[:half]
    other[...] = total[half:]


def query_halves(first, blocks, weight):
    depth, width = weight.shape
    half = 4 * blocks[0].shape[0]
    cuts = pieces(depth, 640)
    return pl.pallas_call(
        lambda *refs: query_kernel(cuts, *refs),
        out_shape=[jax.ShapeDtypeStruct((half, width), F32)] * 2,
        in_specs=[SMEM] + [VMEM] * 8 + [ANY],
        out_specs=[VMEM] * 2,
        scratch_shapes=[
            pltpu.VMEM((2 * half, depth), BF16),
            pltpu.VMEM((depth, width), BF16),
            pltpu.SemaphoreType.DMA((len(cuts),)),
        ],
        compiler_params=pltpu.CompilerParams(vmem_limit_bytes=16 << 20),
        name="query",
    )(first, *blocks, weight)


def gate_up_kernel(cuts, *rest):
    blocks, (gate_w, up_w, gate, up, gate_s, up_s, left, gate_h, up_h, sems) = rest[:8], rest[8:]
    copies = []
    for i, (s, n) in enumerate(cuts):
        for j, (source, held) in enumerate(((gate_w, gate_h), (up_w, up_h))):
            copies.append(
                pltpu.make_async_copy(
                    source.at[pl.ds(s, n)], held.at[pl.ds(s, n)], sems.at[2 * i + j]
                )
            )
    for copy in copies:
        copy.start()
    left[...] = jnp.concatenate([b[...] for b in blocks], axis=0)
    for i, (s, n) in enumerate(cuts):
        for j, (held, full, short) in enumerate(((gate_h, gate, gate_s), (up_h, up, up_s))):
            copies[2 * i + j].wait()
            result = lax.dot_general(
                left[...], held[pl.ds(s, n), :], NT, preferred_element_type=F32
            )
            full[:, s : s + n] = result
            short[:, s : s + n] = result.astype(BF16)


def gate_up(blocks, gate_t, up_t):
    units, depth = gate_t.shape
    rows = 8 * blocks[0].shape[0]
    cuts = pieces(units, 512)
    return pl.pallas_call(
        lambda *refs: gate_up_kernel(cuts, *refs),
        out_shape=[jax.ShapeDtypeStruct((rows, units), F32)] * 2
        + [jax.ShapeDtypeStruct((rows, units), BF16)] * 2,
        in_specs=[VMEM] * 8 + [ANY] * 2,
        out_specs=[VMEM] * 4,
        scratch_shapes=[
            pltpu.VMEM((rows, depth), BF16),
            pltpu.VMEM((units, depth), BF16),
            pltpu.VMEM((units, depth), BF16),
            pltpu.SemaphoreType.DMA((2 * len(cuts),)),
        ],
        compiler_params=pltpu.CompilerParams(vmem_limit_bytes=32 << 20),
        name="gate_up",
    )(*blocks, gate_t, up_t)


def down_kernel(cuts, gate, up, gate_r, up_r, weight, *rest):
    kept, sent, (held, sems) = rest[:4], rest[4:8], rest[8:]
    copies = [
        pltpu.make_async_copy(weight.at[:, pl.ds(s, n)], held.at[:, pl.ds(s, n)], sems.at[i])
        for i, (s, n) in enumerate(cuts)
    ]
    for copy in copies:
        copy.start()
    g = gate[...] + gate_r[...].astype(F32)
    u = up[...] + up_r[...].astype(F32)
    left = (jax.nn.gelu(g, approximate=True) * u).astype(BF16)
    for copy, (s, n) in zip(copies, cuts):
        copy.wait()
        store_blocks(dot(left, held[:, pl.ds(s, n)]), kept, sent, s, n)


def down(gate, up, gate_r, up_r, weight):
    units, width = weight.shape
    cuts = pieces(width, 512)
    outs = pl.pallas_call(
        lambda *refs: down_kernel(cuts, *refs),
        out_shape=block_shapes(gate.shape[0] // 8, width),
        in_specs=[VMEM] * 4 + [ANY],
        out_specs=[VMEM] * 8,
        scratch_shapes=[
            pltpu.VMEM((units, width), BF16),
            pltpu.SemaphoreType.DMA((len(cuts),)),
        ],
        compiler_params=pltpu.CompilerParams(vmem_limit_bytes=32 << 20),
        name="down",
    )(gate, up, gate_r, up_r, weight)
    return outs[:4], outs[4:]


def attend_kernel(own, block, *refs):
    if own:
        low, lengths, query_a, query_b, pair_a, pair_b, keys, values, out = refs[:9]
    else:
        low, query_a, query_b, keys, values, out = refs[:6]
    held_k, held_v, sems = refs[-3:]
    heads, rows, width, slots = held_k.shape
    pairs = heads // 2

    def copies(i):
        both = pl.ds(2 * i, 2)
        return (
            pltpu.make_async_copy(keys.at[both], held_k.at[both], sems.at[0, i]),
            pltpu.make_async_copy(values.at[both], held_v.at[both], sems.at[1, i]),
        )

    for i in range(pairs):
        for copy in copies(i):
            copy.start()
    spread = block * width
    row = lax.broadcasted_iota(jnp.int32, (block, spread), 0)
    lane = lax.broadcasted_iota(jnp.int32, (block, spread), 1)
    diagonal = lane // width == row
    places = [pl.multiple_of((b ^ low[0]) * block, block) for b in range(rows // block)]
    if own:
        lens = jnp.concatenate([lengths[pl.ds(p, block), :] for p in places], axis=0)
        valid = lax.broadcasted_iota(jnp.int32, (rows, slots), 1) < lens

    def step(i, carry):
        cols = pl.ds(pl.multiple_of(i * 2 * width, 2 * width), 2 * width)
        both = (query_a[:, cols] + query_b[:, cols]).astype(BF16)
        for copy in copies(i):
            copy.wait()
        mixes = []
        for e in range(2):
            h = 2 * i + e
            query = both[:, e * width : (e + 1) * width]
            scores = []
            for b, place in enumerate(places):
                some = query[b * block : (b + 1) * block]
                wide = jnp.concatenate([some] * block, axis=1)
                wide = jnp.where(diagonal, wide, jnp.zeros_like(wide))
                key = held_k[h, pl.ds(place, block)].reshape(spread, slots)
                scores.append(dot(wide, key))
            scores = jnp.concatenate(scores, axis=0)
            if own:
                hcols = pl.ds(pl.multiple_of(h * 2 * width, 2 * width), 2 * width)
                new = (pair_a[:, hcols] + pair_b[:, hcols]).astype(BF16).astype(F32)
                own_score = jnp.sum(query.astype(F32) * new[:, :width], axis=1, keepdims=True)
                scores = jnp.where(valid, scores, -1e30)
                top = jnp.maximum(jnp.max(scores, axis=1, keepdims=True), own_score)
                expo = jnp.where(valid, jnp.exp(scores - top), 0.0)
                own_expo = jnp.exp(own_score - top)
                total = jnp.sum(expo, axis=1, keepdims=True) + own_expo
                own_prob = (own_expo / total).astype(BF16).astype(F32)
            else:
                top = jnp.max(scores, axis=1, keepdims=True)
                expo = jnp.exp(scores - top)
                total = jnp.sum(expo, axis=1, keepdims=True)
            probs = (expo / total).astype(BF16)
            mixed = []
            for b, place in enumerate(places):
                value = held_v[h, pl.ds(place, block)].reshape(spread, slots)
                wide = lax.dot_general(
                    probs[b * block : (b + 1) * block], value, NT, preferred_element_type=F32
                )
                wide = jnp.where(diagonal, wide, 0.0)
                tiles = [wide[:, j * 2 * width : (j + 1) * 2 * width] for j in range(block // 2)]
                while len(tiles) > 1:
                    tiles = [a + c for a, c in zip(tiles[::2], tiles[1::2])]
                mixed.append(tiles[0][:, :width] + tiles[0][:, width:])
            mixed = jnp.concatenate(mixed, axis=0)
            if own:
                mixed = mixed + own_prob * new[:, width:]
            mixes.append(mixed)
        out[:, cols] = jnp.concatenate(mixes, axis=1).astype(BF16)
        return carry

    lax.fori_loop(0, pairs, step, 0)


def attend(low, lengths, query, pair, keys, values):
    own = pair is not None
    operands = [low]
    if own:
        operands += [lengths]
    operands += list(query)
    if own:
        operands += list(pair)
    heads, rows, width, slots = keys.shape
    return pl.pallas_call(
        lambda *refs: attend_kernel(own, rows // 4, *refs),
        out_shape=jax.ShapeDtypeStruct((rows, heads * width), BF16),
        in_specs=[SMEM] + [VMEM] * (len(operands) - 1) + [ANY, ANY],
        out_specs=VMEM,
        scratch_shapes=[
            pltpu.VMEM(keys.shape, BF16),
            pltpu.VMEM(values.shape, BF16),
            pltpu.SemaphoreType.DMA((2, heads // 2)),
        ],
        compiler_params=pltpu.CompilerParams(vmem_limit_bytes=32 << 20),
        name="self_attend" if own else "cross_attend",
    )(*operands, keys, values)


def per_device_eight(
    x_in,
    lengths,
    self_gain,
    cross_gain,
    ffn_gain,
    final_gain,
    self_query,
    self_kv,
    self_out,
    cross_query,
    cross_out,
    ffn_gate,
    ffn_up,
    ffn_down,
    self_keys,
    self_values,
    cross_keys,
    cross_values,
):
    index = lax.axis_index("gx")
    first = (lax.axis_index("gy") ^ (index // 4)).astype(jnp.int32).reshape(1)
    low = (index & 3).astype(jnp.int32).reshape(1)
    half = self_keys.shape[1]
    lengths = jnp.broadcast_to(lengths[:, None], (half, self_keys.shape[3]))

    def other_core(value):
        return swap(value, "gy", 1, 2)

    def update(stream, outs):
        return (stream.astype(F32) + scatter_sum(*outs)).astype(BF16)

    def project_heads(stream, heads, weight):
        return update(stream, heads_out(first, heads, other_core(heads), weight.T))

    stream = x_in
    blocks = gather_blocks(normalize(stream, self_gain))
    lower, upper = jnp.concatenate(blocks[:4], axis=0), jnp.concatenate(blocks[4:], axis=0)
    swapped = first[0] == 1
    normed = jnp.concatenate(
        [jnp.where(swapped, upper, lower), jnp.where(swapped, lower, upper)], axis=0
    )
    query_part = dot(normed, self_query)
    pair_part = dot(normed, self_kv.reshape(self_kv.shape[0], -1))
    query = query_part[:half], other_core(query_part[half:])
    pair = pair_part[:half], other_core(pair_part[half:])
    heads = attend(low, lengths, query, pair, self_keys, self_values)
    stream = project_heads(stream, heads, self_out)

    blocks = gather_blocks(normalize(stream, cross_gain))
    mine, other = query_halves(first, blocks, cross_query)
    heads = attend(low, None, (mine, other_core(other)), None, cross_keys, cross_values)
    stream = project_heads(stream, heads, cross_out)

    blocks = gather_blocks(normalize(stream, ffn_gain))
    gate, up, gate_s, up_s = gate_up(blocks, ffn_gate.T, ffn_up.T)
    stream = update(stream, down(gate, up, other_core(gate_s), other_core(up_s), ffn_down))
    return normalize(stream, final_gain)


def softmax_mix(scores, own_score, cache_values, own_value):
    top = jnp.max(scores, axis=2)
    if own_score is not None:
        top = jnp.maximum(top, own_score)
    expo = jnp.exp(scores - top[:, :, None])
    totals = jnp.sum(expo, axis=2)
    if own_score is not None:
        own_expo = jnp.exp(own_score - top)
        totals = totals + own_expo
    probs = (expo / totals[:, :, None]).astype(BF16)
    mixed = jnp.einsum("hbs,hbds->bhd", probs, cache_values, preferred_element_type=F32)
    if own_score is not None:
        own_prob = (own_expo / totals).astype(BF16).T.astype(F32)
        mixed = mixed + own_prob[:, :, None] * own_value.astype(F32)
    return mixed.astype(BF16).reshape(mixed.shape[0], -1)


def per_device_any(
    x_in,
    lengths,
    self_gain,
    cross_gain,
    ffn_gain,
    final_gain,
    self_query,
    self_kv,
    self_out,
    cross_query,
    cross_out,
    ffn_gate,
    ffn_up,
    ffn_down,
    self_keys,
    self_values,
    cross_keys,
    cross_values,
):
    heads_here = self_query.shape[1] // DK
    rows_here = self_keys.shape[1]

    def half_sum(partial):
        total = lax.psum_scatter(partial, "gy", scatter_dimension=0, tiled=True).astype(BF16)
        return total.reshape(rows_here, heads_here, -1)

    def gather(stream, gain):
        return lax.all_gather(normalize(stream, gain), "gx", axis=0, tiled=True)

    def update(stream, left, weight):
        summed = lax.psum_scatter(dot(left, weight), "gx", scatter_dimension=0, tiled=True)
        return (stream.astype(F32) + summed).astype(BF16)

    def both_halves(heads):
        return lax.all_gather(heads, "gy", axis=0, tiled=True)

    def score(query, keys):
        return jnp.einsum("bhd,hbds->hbs", query, keys, preferred_element_type=F32)

    stream = x_in
    normed = gather(stream, self_gain)
    query = half_sum(dot(normed, self_query))
    pair = half_sum(dot(normed, self_kv.reshape(self_kv.shape[0], -1)))
    scores = score(query, self_keys)
    slots = lax.broadcasted_iota(jnp.int32, (1,) + scores.shape[1:], 2)
    scores = jnp.where(slots < lengths[None, :, None], scores, -jnp.inf)
    own_score = jnp.einsum("bhd,bhd->hb", query, pair[:, :, :DK], preferred_element_type=F32)
    heads = softmax_mix(scores, own_score, self_values, pair[:, :, DK:])
    stream = update(stream, both_halves(heads), self_out)

    query = half_sum(dot(gather(stream, cross_gain), cross_query))
    heads = softmax_mix(score(query, cross_keys), None, cross_values, None)
    stream = update(stream, both_halves(heads), cross_out)

    normed = gather(stream, ffn_gain)
    gate, up = dot(normed, ffn_gate), dot(normed, ffn_up)
    gate = gate + swap(gate.astype(BF16), "gy", 1, 2).astype(F32)
    up = up + swap(up.astype(BF16), "gy", 1, 2).astype(F32)
    hidden = (jax.nn.gelu(gate, approximate=True) * up).astype(BF16)
    return normalize(update(stream, hidden, ffn_down), final_gain)


def solution(mesh):
    eight = mesh.shape["gx"] == 8 and mesh.shape["gy"] == 2
    return jax.shard_map(
        per_device_eight if eight else per_device_any,
        mesh=mesh,
        in_specs=(
            P(("groups", "gx"), "gy"),
            P(("groups", "gy")),
            P("gy"),
            P("gy"),
            P("gy"),
            P("gy"),
            P("gy", "gx"),
            P("gy", "gx", None),
            P("gx", "gy"),
            P("gy", "gx"),
            P("gx", "gy"),
            P("gy", "gx"),
            P("gy", "gx"),
            P("gx", "gy"),
            P("gx", ("groups", "gy"), None, None),
            P("gx", ("groups", "gy"), None, None),
            P("gx", ("groups", "gy"), None, None),
            P("gx", ("groups", "gy"), None, None),
        ),
        out_specs=P(("groups", "gx"), "gy"),
        check_vma=False,
    )
```

```python
import jax
import jax.numpy as jnp
from jax import lax
from jax.experimental import pallas as pl
from jax.experimental.pallas import tpu as pltpu
from jax.sharding import PartitionSpec as P

D = 4672
DK = 64
F32 = jnp.float32
BF16 = jnp.bfloat16
VMEM = pl.BlockSpec(memory_space=pltpu.VMEM)
NT = (((1,), (1,)), ((), ()))


def swap(value, axis, mask, size):
    return lax.ppermute(value, axis, [(i, i ^ mask) for i in range(size)])


def dot(left, right):
    return jnp.dot(left, right, preferred_element_type=F32)


def pieces(total, step):
    starts = list(range(0, total, step))
    if total - starts[-1] < step // 8 and len(starts) > 1:
        starts.pop()
    return [(s, e - s) for s, e in zip(starts, starts[1:] + [total])]


def norm_kernel(stream, mine, other, gain, out):
    inverse = lax.rsqrt((mine[...] + other[...]) / D + 1e-06)
    out[...] = (stream[...].astype(F32) * inverse * gain[...]).astype(BF16)


def norm_ahead(stream, gain):
    stream_f = stream.astype(F32)
    squares = jnp.sum(stream_f * stream_f, axis=1, keepdims=True)
    return pl.pallas_call(
        norm_kernel,
        out_shape=jax.ShapeDtypeStruct(stream.shape, BF16),
        in_specs=[VMEM] * 4,
        out_specs=VMEM,
        compiler_params=pltpu.CompilerParams(vmem_limit_bytes=2 << 20),
        cost_estimate=pl.CostEstimate(flops=30_000_000_000, bytes_accessed=60 << 20, transcendentals=0),
        name="norm",
    )(stream, squares, swap(squares, "gy", 1, 2), gain[None, :])


def normalize(stream, gain):
    stream_f = stream.astype(F32)
    squares = jnp.sum(stream_f * stream_f, axis=1, keepdims=True)
    squares = squares + swap(squares, "gy", 1, 2)
    inverse = lax.rsqrt(squares / D + 1e-06)
    return (stream_f * inverse * gain[None, :]).astype(BF16)


def gather_blocks(block):
    blocks = {0: block}
    for mask in (4, 6, 2):
        blocks[mask] = swap(block, "gx", mask, 8)
    blocks[1] = swap(block, "gx", 1, 8)
    for mask in (4, 2, 6):
        blocks[mask ^ 1] = swap(blocks[mask], "gx", 1, 8)
    return [blocks[p] for p in range(8)]


def scatter_sum(kept, sent):
    pairs = {}
    for k in (3, 2, 1, 0):
        pairs[k] = kept[k] + swap(sent[k], "gx", 1, 8).astype(F32)
    total = pairs[0]
    for k in (3, 2, 1):
        total = total + swap(pairs[k].astype(BF16), "gx", 2 * k, 8).astype(F32)
    return total


def store_blocks(result, kept, sent, start, length):
    rows = kept[0].shape[0]
    for k in range(4):
        low = 2 * k * rows
        kept[k][:, start : start + length] = result[low : low + rows]
        sent[k][:, start : start + length] = result[low + rows : low + 2 * rows].astype(BF16)


def block_shapes(rows, width):
    return [jax.ShapeDtypeStruct((rows, width), F32)] * 4 + [
        jax.ShapeDtypeStruct((rows, width), BF16)
    ] * 4


def upper_half_mine():
    return (lax.axis_index("gy") ^ (lax.axis_index("gx") // 4)) == 1


def heads_out_kernel(cuts, mine, other, weight, *rest):
    kept, sent = rest[:4], rest[4:8]
    swapped = upper_half_mine()
    a, b = mine[...], other[...]
    left = jnp.concatenate([jnp.where(swapped, b, a), jnp.where(swapped, a, b)], axis=0)
    for s, n in cuts:
        result = lax.dot_general(left, weight[s : s + n, :], NT, preferred_element_type=F32)
        store_blocks(result, kept, sent, s, n)


def heads_out(mine, other, weight_t):
    width = weight_t.shape[0]
    cuts = pieces(width, 512)
    outs = pl.pallas_call(
        lambda *refs: heads_out_kernel(cuts, *refs),
        out_shape=block_shapes(mine.shape[0] // 4, width),
        in_specs=[VMEM] * 3,
        out_specs=[VMEM] * 8,
        compiler_params=pltpu.CompilerParams(vmem_limit_bytes=12 << 20),
        name="heads_out",
    )(mine, other, weight_t)
    return outs[:4], outs[4:]


def arranged(blocks):
    swapped = upper_half_mine()
    low = jnp.concatenate([b[...] for b in blocks[:4]], axis=0)
    high = jnp.concatenate([b[...] for b in blocks[4:]], axis=0)
    return jnp.concatenate([jnp.where(swapped, high, low), jnp.where(swapped, low, high)], axis=0)


def arrange_kernel(*refs):
    refs[8][...] = arranged(refs[:8])


def arrange(blocks):
    rows, width = blocks[0].shape
    return pl.pallas_call(
        arrange_kernel,
        out_shape=jax.ShapeDtypeStruct((8 * rows, width), BF16),
        in_specs=[VMEM] * 8,
        out_specs=VMEM,
        compiler_params=pltpu.CompilerParams(vmem_limit_bytes=4 << 20),
        name="arrange",
    )(*blocks)


def query_kernel(*refs):
    weight, mine, other = refs[8:]
    total = dot(arranged(refs[:8]), weight[...])
    half = mine.shape[0]
    mine[...] = total[:half]
    other[...] = total[half:]


def query_halves(blocks, weight):
    half = 4 * blocks[0].shape[0]
    return pl.pallas_call(
        query_kernel,
        out_shape=[jax.ShapeDtypeStruct((half, weight.shape[1]), F32)] * 2,
        in_specs=[VMEM] * 9,
        out_specs=[VMEM] * 2,
        compiler_params=pltpu.CompilerParams(vmem_limit_bytes=12 << 20),
        name="query",
    )(*blocks, weight)


def gate_up_kernel(cuts, *refs):
    blocks, (gate_w, up_w, gate, up, gate_s, up_s) = refs[:8], refs[8:]
    left = jnp.concatenate([b[...] for b in blocks], axis=0)
    for weight, full, short in ((gate_w, gate, gate_s), (up_w, up, up_s)):
        for s, n in cuts:
            result = lax.dot_general(left, weight[s : s + n, :], NT, preferred_element_type=F32)
            full[:, s : s + n] = result
            short[:, s : s + n] = result.astype(BF16)


def gate_up(blocks, gate_t, up_t):
    units = gate_t.shape[0]
    rows = 8 * blocks[0].shape[0]
    cuts = pieces(units, 256)
    return pl.pallas_call(
        lambda *refs: gate_up_kernel(cuts, *refs),
        out_shape=[jax.ShapeDtypeStruct((rows, units), F32)] * 2
        + [jax.ShapeDtypeStruct((rows, units), BF16)] * 2,
        in_specs=[VMEM] * 10,
        out_specs=[VMEM] * 4,
        compiler_params=pltpu.CompilerParams(vmem_limit_bytes=24 << 20),
        name="gate_up",
    )(*blocks, gate_t, up_t)


def down_kernel(cuts, gate, up, gate_r, up_r, weight, *rest):
    kept, sent = rest[:4], rest[4:8]
    g = gate[...] + gate_r[...].astype(F32)
    u = up[...] + up_r[...].astype(F32)
    left = (jax.nn.gelu(g, approximate=True) * u).astype(BF16)
    for s, n in cuts:
        store_blocks(dot(left, weight[:, s : s + n]), kept, sent, s, n)


def down(gate, up, gate_r, up_r, weight):
    width = weight.shape[1]
    cuts = pieces(width, 512)
    outs = pl.pallas_call(
        lambda *refs: down_kernel(cuts, *refs),
        out_shape=block_shapes(gate.shape[0] // 8, width),
        in_specs=[VMEM] * 5,
        out_specs=[VMEM] * 8,
        compiler_params=pltpu.CompilerParams(vmem_limit_bytes=20 << 20),
        name="down",
    )(gate, up, gate_r, up_r, weight)
    return outs[:4], outs[4:]


def attend_kernel(own, block, *refs):
    if own:
        lengths, query_a, query_b, pair_a, pair_b, held_k, held_v, out = refs
    else:
        query_a, query_b, held_k, held_v, out = refs
    heads, rows, width, slots = held_k.shape
    low = lax.axis_index("gx") & 3
    pairs = heads // 2

    spread = block * width
    row = lax.broadcasted_iota(jnp.int32, (block, spread), 0)
    lane = lax.broadcasted_iota(jnp.int32, (block, spread), 1)
    diagonal = lane // width == row
    places = [pl.multiple_of((b ^ low) * block, block) for b in range(rows // block)]
    if own:
        lens = jnp.concatenate([lengths[pl.ds(p, block), :] for p in places], axis=0)
        valid = lax.broadcasted_iota(jnp.int32, (rows, slots), 1) < lens

    def softmax(scores, own_score):
        if own:
            scores = jnp.where(valid, scores, -1e30)
        top = jnp.max(scores, axis=1, keepdims=True)
        if own:
            top = jnp.maximum(top, own_score)
        expo = jnp.exp(scores - top)
        if own:
            expo = jnp.where(valid, expo, 0.0)
        total = jnp.sum(expo, axis=1, keepdims=True)
        if not own:
            return (expo / total).astype(BF16), None
        own_expo = jnp.exp(own_score - top)
        total = total + own_expo
        return (expo / total).astype(BF16), (own_expo / total).astype(BF16).astype(F32)

    def paired(held, i, place):
        return jnp.concatenate(
            [held[2 * i + e, pl.ds(place, block)].reshape(spread, slots) for e in range(2)], axis=1
        )

    def step(i, carry):
        cols = pl.ds(pl.multiple_of(i * 2 * width, 2 * width), 2 * width)
        both = (query_a[:, cols] + query_b[:, cols]).astype(BF16)
        queries = [both[:, e * width : (e + 1) * width] for e in range(2)]
        news, own_scores = [None, None], [None, None]
        if own:
            for e in range(2):
                hcols = pl.ds(pl.multiple_of((2 * i + e) * 2 * width, 2 * width), 2 * width)
                news[e] = (pair_a[:, hcols] + pair_b[:, hcols]).astype(BF16).astype(F32)
                own_scores[e] = jnp.sum(
                    queries[e].astype(F32) * news[e][:, :width], axis=1, keepdims=True
                )
        scores = [[], []]
        for b, place in enumerate(places):
            wides = []
            for e in range(2):
                wide = jnp.concatenate([queries[e][b * block : (b + 1) * block]] * block, axis=1)
                wides.append(jnp.where(diagonal, wide, jnp.zeros_like(wide)))
            result = dot(jnp.concatenate(wides, axis=0), paired(held_k, i, place))
            scores[0].append(result[:block, :slots])
            scores[1].append(result[block:, slots:])
        probs, own_probs = [None, None], [None, None]
        for e in range(2):
            probs[e], own_probs[e] = softmax(jnp.concatenate(scores[e], axis=0), own_scores[e])
        mixes = [[], []]
        for b, place in enumerate(places):
            parts = [p[b * block : (b + 1) * block] for p in probs]
            none = jnp.zeros_like(parts[0])
            left = jnp.concatenate(
                [
                    jnp.concatenate([parts[0], none], axis=1),
                    jnp.concatenate([none, parts[1]], axis=1),
                ],
                axis=0,
            )
            result = lax.dot_general(
                left, paired(held_v, i, place), NT, preferred_element_type=F32
            )
            for e in range(2):
                wide = jnp.where(diagonal, result[e * block : (e + 1) * block], 0.0)
                tiles = [wide[:, j * 2 * width : (j + 1) * 2 * width] for j in range(block // 2)]
                while len(tiles) > 1:
                    tiles = [a + c for a, c in zip(tiles[::2], tiles[1::2])]
                mixes[e].append(tiles[0][:, :width] + tiles[0][:, width:])
        mixes = [jnp.concatenate(m, axis=0) for m in mixes]
        if own:
            mixes = [m + p * n[:, width:] for m, p, n in zip(mixes, own_probs, news)]
        out[:, cols] = jnp.concatenate(mixes, axis=1).astype(BF16)
        return carry

    lax.fori_loop(0, pairs, step, 0)


def attend(lengths, query, pair, keys, values):
    own = pair is not None
    operands = ([lengths] if own else []) + list(query) + (list(pair) if own else [])
    operands += [keys, values]
    heads, rows, width, slots = keys.shape
    return pl.pallas_call(
        lambda *refs: attend_kernel(own, rows // 4, *refs),
        out_shape=jax.ShapeDtypeStruct((rows, heads * width), BF16),
        in_specs=[VMEM] * len(operands),
        out_specs=VMEM,
        compiler_params=pltpu.CompilerParams(vmem_limit_bytes=24 << 20),
        name="self_attend" if own else "cross_attend",
    )(*operands)


def per_device_eight(
    x_in,
    lengths,
    self_gain,
    cross_gain,
    ffn_gain,
    final_gain,
    self_query,
    self_kv,
    self_out,
    cross_query,
    cross_out,
    ffn_gate,
    ffn_up,
    ffn_down,
    self_keys,
    self_values,
    cross_keys,
    cross_values,
):
    half = self_keys.shape[1]
    lengths = jnp.broadcast_to(lengths[:, None], (half, self_keys.shape[3]))

    def other_core(value):
        return swap(value, "gy", 1, 2)

    def update(stream, outs):
        return (stream.astype(F32) + scatter_sum(*outs)).astype(BF16)

    def project_heads(stream, heads, weight):
        return update(stream, heads_out(heads, other_core(heads), weight.T))

    stream = x_in
    normed = arrange(gather_blocks(norm_ahead(stream, self_gain)))
    query_part = dot(normed, self_query)
    pair_part = dot(normed, self_kv.reshape(self_kv.shape[0], -1))
    query = query_part[:half], other_core(query_part[half:])
    pair = pair_part[:half], other_core(pair_part[half:])
    heads = attend(lengths, query, pair, self_keys, self_values)
    stream = project_heads(stream, heads, self_out)

    blocks = gather_blocks(norm_ahead(stream, cross_gain))
    mine, other = query_halves(blocks, cross_query)
    heads = attend(None, (mine, other_core(other)), None, cross_keys, cross_values)
    stream = project_heads(stream, heads, cross_out)

    blocks = gather_blocks(norm_ahead(stream, ffn_gain))
    gate, up, gate_s, up_s = gate_up(blocks, ffn_gate.T, ffn_up.T)
    stream = update(stream, down(gate, up, other_core(gate_s), other_core(up_s), ffn_down))
    return normalize(stream, final_gain)


def softmax_mix(scores, own_score, cache_values, own_value):
    top = jnp.max(scores, axis=2)
    if own_score is not None:
        top = jnp.maximum(top, own_score)
    expo = jnp.exp(scores - top[:, :, None])
    totals = jnp.sum(expo, axis=2)
    if own_score is not None:
        own_expo = jnp.exp(own_score - top)
        totals = totals + own_expo
    probs = (expo / totals[:, :, None]).astype(BF16)
    mixed = jnp.einsum("hbs,hbds->bhd", probs, cache_values, preferred_element_type=F32)
    if own_score is not None:
        own_prob = (own_expo / totals).astype(BF16).T.astype(F32)
        mixed = mixed + own_prob[:, :, None] * own_value.astype(F32)
    return mixed.astype(BF16).reshape(mixed.shape[0], -1)


def per_device_any(
    x_in,
    lengths,
    self_gain,
    cross_gain,
    ffn_gain,
    final_gain,
    self_query,
    self_kv,
    self_out,
    cross_query,
    cross_out,
    ffn_gate,
    ffn_up,
    ffn_down,
    self_keys,
    self_values,
    cross_keys,
    cross_values,
):
    heads_here = self_query.shape[1] // DK
    rows_here = self_keys.shape[1]

    def half_sum(partial):
        total = lax.psum_scatter(partial, "gy", scatter_dimension=0, tiled=True).astype(BF16)
        return total.reshape(rows_here, heads_here, -1)

    def gather(stream, gain):
        return lax.all_gather(normalize(stream, gain), "gx", axis=0, tiled=True)

    def update(stream, left, weight):
        summed = lax.psum_scatter(dot(left, weight), "gx", scatter_dimension=0, tiled=True)
        return (stream.astype(F32) + summed).astype(BF16)

    def both_halves(heads):
        return lax.all_gather(heads, "gy", axis=0, tiled=True)

    def score(query, keys):
        return jnp.einsum("bhd,hbds->hbs", query, keys, preferred_element_type=F32)

    stream = x_in
    normed = gather(stream, self_gain)
    query = half_sum(dot(normed, self_query))
    pair = half_sum(dot(normed, self_kv.reshape(self_kv.shape[0], -1)))
    scores = score(query, self_keys)
    slots = lax.broadcasted_iota(jnp.int32, (1,) + scores.shape[1:], 2)
    scores = jnp.where(slots < lengths[None, :, None], scores, -jnp.inf)
    own_score = jnp.einsum("bhd,bhd->hb", query, pair[:, :, :DK], preferred_element_type=F32)
    heads = softmax_mix(scores, own_score, self_values, pair[:, :, DK:])
    stream = update(stream, both_halves(heads), self_out)

    query = half_sum(dot(gather(stream, cross_gain), cross_query))
    heads = softmax_mix(score(query, cross_keys), None, cross_values, None)
    stream = update(stream, both_halves(heads), cross_out)

    normed = gather(stream, ffn_gain)
    gate, up = dot(normed, ffn_gate), dot(normed, ffn_up)
    gate = gate + swap(gate.astype(BF16), "gy", 1, 2).astype(F32)
    up = up + swap(up.astype(BF16), "gy", 1, 2).astype(F32)
    hidden = (jax.nn.gelu(gate, approximate=True) * up).astype(BF16)
    return normalize(update(stream, hidden, ffn_down), final_gain)


def solution(mesh):
    eight = mesh.shape["gx"] == 8 and mesh.shape["gy"] == 2
    return jax.shard_map(
        per_device_eight if eight else per_device_any,
        mesh=mesh,
        in_specs=(
            P(("groups", "gx"), "gy"),
            P(("groups", "gy")),
            P("gy"),
            P("gy"),
            P("gy"),
            P("gy"),
            P("gy", "gx"),
            P("gy", "gx", None),
            P("gx", "gy"),
            P("gy", "gx"),
            P("gx", "gy"),
            P("gy", "gx"),
            P("gy", "gx"),
            P("gx", "gy"),
            P("gx", ("groups", "gy"), None, None),
            P("gx", ("groups", "gy"), None, None),
            P("gx", ("groups", "gy"), None, None),
            P("gx", ("groups", "gy"), None, None),
        ),
        out_specs=P(("groups", "gx"), "gy"),
        check_vma=False,
    )
```
